512 devices in a mesh: row: 32 (over z, x_lo), col: 16 (over x_hi, y, core).
Axes of the slice: x: 4 (x_hi: 2, x_lo: 2; x = x_hi * 2 + x_lo), y: 4, z: 16, core: 2. Of those that a mesh axis runs over, the one named last changes fastest.
Arguments:
- vectors: float32 [64, 65536], P(None, ('row', 'col')), may hold values from -6 to 6
- blocks: bfloat16 [32, 16, 152, 128, 128], P('row', 'col'), may hold values from -0.0390625 to 0.0390625
- slot_block_rows: int32 [32, 16, 152], P('row', 'col'), may hold values from 0 to 15
- slot_block_columns: int32 [32, 16, 152], P('row', 'col'), may hold values from 0 to 31
- counts: int32 [32, 16], P('row', 'col'), may hold values from 38 to 152, as said below
Outputs:
- filtered: float32 [64, 65536], P(None, ('row', 'col'))
The draws below stay inside these ranges and needn't reach their ends.
Inputs may be any that keep to these rules, and one draw needn't show every extreme that they name: `counts`: slots at or after a device's count carry no block.
All inputs are finite; a program needn't handle non-finite values.
Results may differ from the reference program's by a relative error of at most 0.023.
Values may be sent and summed in bfloat16 or wider, within the bound.
No kernel may reach another device: no remote copies, remote signals or barrier semaphores. Data moves between devices by JAX's collectives and lax.ppermute only.
A program may use at most 64 MiB of HBM per device.

```python
import jax
import jax.numpy as jnp
from jax import lax

ORBITAL_COUNT = 128
K = 64
DEVICE_SLOTS = 152
DEGREE = 3
N = 65536
SLAB_BLOCK_ROWS = 16
SLAB_BLOCK_COLS = 32
NBLK = 512
N_ROW = 32
N_COL = 16


def draw_counts(key, part):
    key = jax.random.fold_in(key, 11)
    leading_entry, second = jax.random.split(key)
    start_offset = jax.random.randint(leading_entry, (N_ROW * N_COL,), DEVICE_SLOTS // 4, DEVICE_SLOTS + 1).astype(jnp.int32)
    busiest_device = jax.random.randint(second, (), 0, N_ROW * N_COL).astype(jnp.int32)
    slot_positions = jnp.arange(N_ROW * N_COL, dtype=jnp.int32)
    start_offset = jnp.where(slot_positions == busiest_device, jnp.int32(DEVICE_SLOTS), start_offset)
    return start_offset.reshape(N_ROW, N_COL)


def with_ends(array, key, least, largest):
    extent = array.shape
    spot = [jax.random.randint(jax.random.fold_in(key, axis), (), 0, extent[axis]) for axis in range(len(extent))]
    array = array.at[tuple(spot)].set(least)
    longest = extent.index(max(extent))
    spot[longest] = (spot[longest] + 1) % extent[longest]
    return array.at[tuple(spot)].set(largest)


def shard_levels(own_key, shape, pieces, low, high):
    gain = 1.0
    for position, blocks in pieces:
        heights = jax.random.uniform(jax.random.fold_in(jax.random.fold_in(own_key, 6), position), (blocks,), jnp.float32, low / len(pieces), high / len(pieces))
        gain = gain * jnp.repeat(jnp.exp(heights), shape[position] // blocks).reshape((-1,) + (1,) * (len(shape) - 1 - position))
    return gain


def centred(key, shape, scale, bound, cuts=(), kind=jnp.bfloat16):
    drawn = jax.random.normal(key, shape, jnp.float32) * scale
    if len(cuts) > 0:
        drawn = shard_levels(key, shape, cuts, -0.22, 0.18) * drawn
    return jnp.clip(drawn, min=-bound, max=bound).astype(kind)


def setup_inputs(seed: int = 0) -> dict:
    splits = jax.random.split(jax.random.key(seed), 6)
    vectors = centred(splits[0], (K, N), 1.0, 6.0, ((1, 512),), jnp.float32)
    blocks = centred(splits[1], (N_ROW, N_COL, DEVICE_SLOTS, ORBITAL_COUNT, ORBITAL_COUNT), (ORBITAL_COUNT * N_COL * DEVICE_SLOTS // SLAB_BLOCK_ROWS) ** -0.5, 0.0390625, ((0, 32), (1, 16)))
    slot_block_rows = with_ends(jax.random.randint(splits[2], (N_ROW, N_COL, DEVICE_SLOTS), 0, SLAB_BLOCK_ROWS), jax.random.fold_in(splits[2], 1), 0, SLAB_BLOCK_ROWS - 1).astype(jnp.int32)
    slot_block_columns = with_ends(jax.random.randint(splits[3], (N_ROW, N_COL, DEVICE_SLOTS), 0, SLAB_BLOCK_COLS), jax.random.fold_in(splits[3], 1), 0, SLAB_BLOCK_COLS - 1).astype(jnp.int32)
    counts = draw_counts(jax.random.fold_in(splits[5], 71), 0)
    return {"vectors": vectors, "blocks": blocks, "slot_block_rows": slot_block_rows, "slot_block_columns": slot_block_columns, "counts": counts}


CENTER = 0.25
HALF_WIDTH = 2.0


def hamiltonian(current, blocks, slot_block_rows, slot_block_columns, counts):
    width = current.shape[0]
    slab_groups = N_ROW // N_COL
    wire = current.astype(jnp.bfloat16).reshape(width, NBLK, ORBITAL_COUNT)
    row_ids = jnp.arange(N_ROW, dtype=jnp.int32)[:, None, None]
    col_ids = jnp.arange(N_COL, dtype=jnp.int32)[None, :, None]
    slot_numbers = jnp.arange(DEVICE_SLOTS, dtype=jnp.int32)[None, None, :]
    global_rows = (row_ids * SLAB_BLOCK_ROWS + slot_block_rows).astype(jnp.int32)
    global_cols = ((col_ids + N_COL * (slot_block_columns // SLAB_BLOCK_ROWS)) * SLAB_BLOCK_ROWS + slot_block_columns % SLAB_BLOCK_ROWS).astype(jnp.int32)
    live = (slot_numbers < counts[:, :, None]) & (global_rows <= global_cols)
    row_range = jnp.arange(SLAB_BLOCK_ROWS, dtype=jnp.int32)
    col_range = jnp.arange(SLAB_BLOCK_COLS, dtype=jnp.int32)

    def one_row(carry, inputs):
        block_entries, rows_here, cols_here, grow_here, gcol_here, live_here = inputs
        block_entries = jnp.where(live_here[:, :, None, None], block_entries, jnp.zeros_like(block_entries)).astype(jnp.float32)
        inputs_col = wire[:, gcol_here, :].astype(jnp.float32)
        products = jnp.einsum('jsab,kjsb->kjsa', block_entries, inputs_col)
        onehot_rows = (rows_here[:, :, None] == row_range).astype(jnp.float32)
        row_part = jnp.einsum('jsr,kjsa->kjra', onehot_rows, products)
        row_part = lax.optimization_barrier(row_part.astype(jnp.bfloat16)).astype(jnp.float32)
        row_sum = jnp.sum(row_part, axis=1)
        inputs_row = wire[:, grow_here, :].astype(jnp.float32)
        products_t = jnp.einsum('jsba,kjsb->kjsa', block_entries, inputs_row)
        onehot_cols = (cols_here[:, :, None] == col_range).astype(jnp.float32)
        col_part = jnp.einsum('jsc,kjsa->kjca', onehot_cols, products_t)
        col_part = lax.optimization_barrier(col_part.astype(jnp.bfloat16)).astype(jnp.float32)
        return carry + col_part, row_sum

    start = jnp.zeros((width, N_COL, SLAB_BLOCK_COLS, ORBITAL_COUNT), jnp.float32)
    col_total, row_sums = lax.scan(one_row, start, (blocks, slot_block_rows, slot_block_columns, global_rows, global_cols, live))
    row_full = jnp.transpose(row_sums, (1, 0, 2, 3)).reshape(width, N)
    col_full = col_total.reshape(width, N_COL, slab_groups, SLAB_BLOCK_ROWS, ORBITAL_COUNT)
    col_full = jnp.transpose(col_full, (0, 2, 1, 3, 4)).reshape(width, N)
    return row_full + col_full


def reference(vectors, blocks, slot_block_rows, slot_block_columns, counts):
    previous = vectors
    current = (hamiltonian(vectors, blocks, slot_block_rows, slot_block_columns, counts) - CENTER * vectors) / HALF_WIDTH
    for degree_step in range(DEGREE - 1):
        image = hamiltonian(current, blocks, slot_block_rows, slot_block_columns, counts)
        following = 2.0 * (image - CENTER * current) / HALF_WIDTH - previous
        previous, current = current, following
    return current
```

```python
import jax
import jax.numpy as jnp
from jax import lax
from jax.experimental import pallas as pl
from jax.experimental.pallas import tpu as pltpu
from jax.sharding import Mesh, PartitionSpec as P

CENTER = 0.25
HALF_WIDTH = 2.0
DEGREE = 3
UNROLL = 4
ROW = ("zh", "zl", "xl")
COL = ("xh", "y", "core")
FAR = "zh"
NEAR = ("zl", "xl")
ALL = ROW + COL


def term_kernel(transposed, sources, targets, x_ref, blocks_ref, out_ref, acc):
    acc[...] = jnp.zeros_like(acc)
    contract = (((1,), (1,)), ((), ())) if transposed else (((1,), (0,)), ((), ()))

    def body(step, carry):
        products = []
        for u in range(UNROLL):
            s = step * UNROLL + u
            products.append(
                lax.dot_general(x_ref[sources[s]], blocks_ref[s], contract, preferred_element_type=jnp.float32)
            )
        for u in range(UNROLL):
            t = targets[step * UNROLL + u]
            acc[t] = acc[t] + products[u]
        return carry

    lax.fori_loop(0, blocks_ref.shape[0] // UNROLL, body, 0)
    out_ref[...] = acc[: out_ref.shape[0]].astype(out_ref.dtype)


def terms(x, blocks, sources, targets, count, transposed):
    slots, size = blocks.shape[:2]
    width = x.shape[1]
    smem = pl.BlockSpec(memory_space=pltpu.SMEM)
    vmem = pl.BlockSpec(memory_space=pltpu.VMEM)
    return pl.pallas_call(
        lambda *refs: term_kernel(transposed, *refs),
        out_shape=jax.ShapeDtypeStruct((count, width, size), jnp.bfloat16),
        in_specs=[smem, smem, vmem, vmem],
        out_specs=vmem,
        scratch_shapes=[pltpu.VMEM((count + 1, width, size), jnp.float32)],
        compiler_params=pltpu.CompilerParams(vmem_limit_bytes=32 * 1024 * 1024),
        cost_estimate=pl.CostEstimate(
            flops=2 * slots * width * size * size, bytes_accessed=2 * slots * size * size, transcendentals=0
        ),
        name="row_terms" if transposed else "col_terms",
    )(sources, targets, x, blocks)


def spread(x, axes, n):
    copies = jnp.broadcast_to(x[None], (n,) + x.shape)
    return lax.all_to_all(copies, axes, 0, 0, tiled=True)


def collect(parts, axes):
    received = lax.all_to_all(parts, axes, 0, 0, tiled=True)
    return jnp.sum(received.astype(jnp.float32), axis=0)


def local(vectors, blocks, slot_block_rows, slot_block_columns, counts):
    width, size = vectors.shape
    blocks = blocks[0, 0]
    rows_here = slot_block_rows[0, 0]
    cols_here = slot_block_columns[0, 0]
    slots = blocks.shape[0]
    n_row, n_col = lax.axis_size(ROW), lax.axis_size(COL)
    n_far, n_near = lax.axis_size(FAR), lax.axis_size(NEAR)
    row, col = lax.axis_index(ROW), lax.axis_index(COL)
    global_rows = row * n_col + rows_here
    global_cols = (col + n_col * (cols_here // n_col)) * n_col + cols_here % n_col
    live = (jnp.arange(slots, dtype=jnp.int32) < counts[0, 0]) & (global_rows <= global_cols)
    cols_at = (cols_here % n_near) * n_far + cols_here // n_near
    row_targets = jnp.where(live, rows_here, n_col)
    col_targets = jnp.where(live, cols_at, n_row)
    swap = [
        ((h * n_col + i) * n_col + j, (h * n_col + j) * n_col + i)
        for h in range(n_row // n_col)
        for i in range(n_col)
        for j in range(n_col)
    ]

    def swapped(x):
        return lax.ppermute(x.astype(jnp.bfloat16), ALL, swap)

    def column_terms(wire):
        row_slab = spread(wire, COL, n_col)
        out = terms(row_slab, blocks, rows_here, col_targets, n_row, False)
        if n_far == 1:
            return collect(out, ROW)
        out = collect(out.reshape(n_near, n_far, width, size), NEAR).astype(jnp.bfloat16)
        return collect(out, FAR)

    def row_terms(wire):
        if n_far == 1:
            col_slab = spread(wire, ROW, n_row)
        else:
            col_slab = spread(spread(wire, FAR, n_far), NEAR, n_near).reshape(n_row, width, size)
        out = terms(col_slab, blocks, cols_at, row_targets, n_col, True)
        return collect(out, COL)

    before = (None, None)
    now = (vectors, swapped(vectors).astype(jnp.float32))
    for step in range(DEGREE):
        col_total = column_terms(now[0].astype(jnp.bfloat16))
        row_total = row_terms(now[1].astype(jnp.bfloat16))
        image = [row_total + swapped(col_total).astype(jnp.float32), None]
        if step < DEGREE - 1:
            image[1] = col_total + swapped(row_total).astype(jnp.float32)
        if step == 0:
            after = [None if h is None else (h - CENTER * x) / HALF_WIDTH for h, x in zip(image, now)]
        else:
            after = [
                None if h is None else 2.0 * (h - CENTER * x) / HALF_WIDTH - b for h, x, b in zip(image, now, before)
            ]
        before, now = now, after
    return now[0]


def solution(mesh):
    split = Mesh(mesh.devices.reshape(4, 4, 2, 2, 4, 2), ALL)
    in_specs = (
        P(None, ALL),
        P(ROW, COL, None, None, None),
        P(ROW, COL, None),
        P(ROW, COL, None),
        P(ROW, COL),
    )
    return jax.shard_map(local, mesh=split, in_specs=in_specs, out_specs=P(None, ALL), check_vma=False)
```

```python
import jax
import jax.numpy as jnp
from jax import lax
from jax.experimental import pallas as pl
from jax.experimental.pallas import tpu as pltpu
from jax.sharding import Mesh, PartitionSpec as P

CENTER = 0.25
HALF_WIDTH = 2.0
DEGREE = 3
CHUNKS = 8
ROW = ("zh", "zl", "xl")
COL = ("xh", "y", "core")
PLANE = ("xl",) + COL
ALL = ROW + COL
N_ZH, N_ZL, N_XL, N_COL = 4, 4, 2, 16
N_HALF = N_ZH * N_ZL * N_XL // N_COL
VMEM = pl.BlockSpec(memory_space=pltpu.VMEM)
SMEM = pl.BlockSpec(memory_space=pltpu.SMEM)
FLOAT = jnp.float32
WIRE = jnp.bfloat16
SMALL, LARGE = 4 << 20, 16 << 20


def places():
    for h in range(N_HALF):
        for b in range(N_COL):
            z, parity = divmod(h * N_COL + b, N_XL)
            yield h, b, z % N_ZL, z // N_ZL, parity


def terms_kernel(rows, cols, row_targets, col_targets, x_ref, blocks, out_ref, col_acc, row_acc):
    slots = blocks.shape[0]
    part = slots // CHUNKS
    width = x_ref.shape[0] * x_ref.shape[3]
    half = x_ref.shape[3]
    col_acc[...] = jnp.zeros_like(col_acc)
    row_acc[...] = jnp.zeros_like(row_acc)

    def chunk(i, carry):
        base = i * part
        for u in range(part):
            s = base + u
            block = blocks[s]
            col = cols[s]
            x_row = x_ref[:, rows[s], N_HALF].reshape(width, block.shape[0])
            x_col = x_ref[:, lax.rem(col, N_COL), lax.div(col, N_COL)].reshape(width, block.shape[0])
            t = col_targets[s]
            col_acc[t] = col_acc[t] + lax.dot_general(x_row, block, (((1,), (0,)), ((), ())), preferred_element_type=FLOAT)
            t = row_targets[s]
            row_acc[t] = row_acc[t] + lax.dot_general(x_col, block, (((1,), (1,)), ((), ())), preferred_element_type=FLOAT)
        return carry

    lax.fori_loop(0, CHUNKS, chunk, 0)
    for k in range(x_ref.shape[0]):
        lines = slice(k * half, (k + 1) * half)
        for h in range(N_HALF):
            out_ref[k, :, h] = col_acc[h * N_COL : (h + 1) * N_COL, lines].astype(WIRE)
        out_ref[k, :, N_HALF] = row_acc[:N_COL, lines].astype(WIRE)


def terms(x, blocks, indices):
    slots, size = blocks.shape[:2]
    width = x.shape[0] * x.shape[3]
    return pl.pallas_call(
        terms_kernel,
        out_shape=jax.ShapeDtypeStruct(x.shape, WIRE),
        in_specs=[SMEM] * 4 + [VMEM, VMEM],
        out_specs=VMEM,
        scratch_shapes=[
            pltpu.VMEM((N_HALF * N_COL + 1, width, size), FLOAT),
            pltpu.VMEM((N_COL + 1, width, size), FLOAT),
        ],
        compiler_params=pltpu.CompilerParams(vmem_limit_bytes=LARGE),
        name="terms",
    )(*indices, x, blocks)


def merge_kernel(got_ref, out_ref, acc):
    for h, b, zl, zh, parity in places():
        acc[zl, zh, parity] = got_ref[0, b, h].astype(FLOAT) + got_ref[1, b, h].astype(FLOAT)
    zh, zl = lax.axis_index("zh"), lax.axis_index("zl")
    for parity in range(N_XL):
        total = got_ref[parity, 0, N_HALF].astype(FLOAT)
        for b in range(1, N_COL):
            total = total + got_ref[parity, b, N_HALF].astype(FLOAT)
        acc[zl, zh, parity] = acc[zl, zh, parity] + total
    out_ref[...] = acc[...].astype(WIRE)


def merge(got):
    shape = (N_ZL, N_ZH, N_XL) + got.shape[3:]
    return pl.pallas_call(
        merge_kernel,
        out_shape=jax.ShapeDtypeStruct(shape, WIRE),
        in_specs=[VMEM],
        out_specs=VMEM,
        scratch_shapes=[pltpu.VMEM(shape, FLOAT)],
        compiler_params=pltpu.CompilerParams(vmem_limit_bytes=SMALL),
        name="merge",
    )(got)


def deal_kernel(all_ref, out_ref):
    zh, zl = lax.axis_index("zh"), lax.axis_index("zl")
    for h, b, b_zl, b_zh, parity in places():
        piece = all_ref[b_zl, b_zh, parity]
        for xl in range(N_XL):
            out_ref[xl, b, h] = piece
    for xl in range(N_XL):
        piece = all_ref[zl, zh, xl]
        for b in range(N_COL):
            out_ref[xl, b, N_HALF] = piece


def deal(pieces):
    return pl.pallas_call(
        deal_kernel,
        out_shape=jax.ShapeDtypeStruct((N_XL, N_COL, N_HALF + 1) + pieces.shape[3:], WIRE),
        in_specs=[VMEM],
        out_specs=VMEM,
        compiler_params=pltpu.CompilerParams(vmem_limit_bytes=SMALL),
        name="deal",
    )(pieces)


def exchange(x, axes):
    return lax.all_to_all(x, axes, 0, 0, tiled=True)


def total(x):
    return jnp.sum(x.astype(FLOAT), axis=0)


def local(vectors, blocks, slot_block_rows, slot_block_columns, counts):
    width, size = vectors.shape
    blocks = blocks[0, 0]
    rows = slot_block_rows[0, 0]
    cols = slot_block_columns[0, 0]
    slots = blocks.shape[0]
    row, col = lax.axis_index(ROW), lax.axis_index(COL)
    zh = lax.axis_index("zh")
    xl = lax.axis_index("xl")
    global_rows = row * N_COL + rows
    global_cols = (col + N_COL * (cols // N_COL)) * N_COL + cols % N_COL
    live = (jnp.arange(slots, dtype=jnp.int32) < counts[0, 0]) & (global_rows <= global_cols)
    indices = (rows, cols, jnp.where(live, rows, N_COL), jnp.where(live, cols, N_HALF * N_COL))

    def plane_sums(now):
        wire = now.astype(WIRE)
        pieces = exchange(jnp.broadcast_to(wire[None], (N_ZL,) + wire.shape), "zl")
        got = exchange(deal(pieces).reshape(N_XL * N_COL, N_HALF + 1, *wire.shape[2:]), PLANE)
        out = terms(got.reshape(N_XL, N_COL, *got.shape[1:]), blocks, indices)
        got = exchange(out.reshape(got.shape), PLANE).reshape(out.shape)
        return total(exchange(merge(got), "zl")).astype(WIRE)

    halves = lax.all_gather(vectors.reshape(N_XL, width // N_XL, size), "xl")[:, xl]
    before, now = None, lax.all_gather(halves, "zh")
    for step in range(DEGREE - 1):
        image = total(lax.all_gather(plane_sums(now), "zh"))
        after = (image - CENTER * now) / HALF_WIDTH
        if step > 0:
            after = 2.0 * (image - CENTER * now) / HALF_WIDTH - before
        before, now = now, after
    image = total(exchange(plane_sums(now), "zh"))
    own = 2.0 * (image - CENTER * now[zh]) / HALF_WIDTH - before[zh]
    return lax.all_gather(own, "xl")[:, xl].reshape(width, size)


def solution(mesh):
    split = Mesh(mesh.devices.reshape(N_ZH, N_ZL, N_XL, 2, 4, 2), ALL)
    in_specs = (
        P(None, ALL),
        P(ROW, COL, None, None, None),
        P(ROW, COL, None),
        P(ROW, COL, None),
        P(ROW, COL),
    )
    return jax.shard_map(local, mesh=split, in_specs=in_specs, out_specs=P(None, ALL), check_vma=False)
```

```python
import jax
import jax.numpy as jnp
from jax import lax
from jax.experimental import pallas as pl
from jax.experimental.pallas import tpu as pltpu
from jax.sharding import Mesh, PartitionSpec as P

CENTER = 0.25
HALF_WIDTH = 2.0
DEGREE = 3
CHUNKS, AHEAD = 8, 2
QUAD = ("z0", "xl")
ROW = ("zh", "z1") + QUAD
COL = ("xh", "y", "core")
UNIT = QUAD + COL
UNITS = ("z1", "zh")
ALL = ROW + COL
N_ZH, N_Z1, N_Q, N_COL = 4, 2, 4, 16
N_HALF = N_ZH * N_Z1 * N_Q // N_COL
VMEM = pl.BlockSpec(memory_space=pltpu.VMEM)
SMEM = pl.BlockSpec(memory_space=pltpu.SMEM)
FLOAT = jnp.float32
WIRE = jnp.bfloat16
SMALL, LARGE = 4 << 20, 52 << 20


def places():
    for h in range(N_HALF):
        for b in range(N_COL):
            zh, rest = divmod(h * N_COL + b, N_Z1 * N_Q)
            yield h, b, rest // N_Q, zh, rest % N_Q


def terms_kernel(index, x_ref, blocks_hbm, out_ref, col_acc, row_acc, blocks, sems):
    slots = blocks.shape[0]
    part = slots // CHUNKS
    width = x_ref.shape[0] * x_ref.shape[3]
    share = x_ref.shape[3]

    def copy(i):
        here = pl.ds(i * part, part)
        return pltpu.make_async_copy(blocks_hbm.at[here], blocks.at[here], sems.at[i])

    for i in range(AHEAD):
        copy(i).start()
    col_acc[...] = jnp.zeros_like(col_acc)
    row_acc[...] = jnp.zeros_like(row_acc)

    def chunk(i, carry):
        base = i * part
        copy(i).wait()

        @pl.when(i + AHEAD < CHUNKS)
        def _():
            copy(i + AHEAD).start()

        for u in range(part):
            s = base + u
            block = blocks[s]
            col = index[slots + s]
            x_row = x_ref[:, index[s], N_HALF].reshape(width, block.shape[0])
            x_col = x_ref[:, lax.rem(col, N_COL), lax.div(col, N_COL)].reshape(width, block.shape[0])
            t = index[3 * slots + s]
            col_acc[t] = col_acc[t] + lax.dot_general(x_row, block, (((1,), (0,)), ((), ())), preferred_element_type=FLOAT)
            t = index[2 * slots + s]
            row_acc[t] = row_acc[t] + lax.dot_general(x_col, block, (((1,), (1,)), ((), ())), preferred_element_type=FLOAT)
        return carry

    lax.fori_loop(0, CHUNKS, chunk, 0)
    for k in range(x_ref.shape[0]):
        lines = slice(k * share, (k + 1) * share)
        for h in range(N_HALF):
            out_ref[k, :, h] = col_acc[h * N_COL : (h + 1) * N_COL, lines].astype(WIRE)
        out_ref[k, :, N_HALF] = row_acc[:N_COL, lines].astype(WIRE)


def terms(x, blocks, index):
    slots, size = blocks.shape[:2]
    width = x.shape[0] * x.shape[3]
    return pl.pallas_call(
        terms_kernel,
        out_shape=jax.ShapeDtypeStruct(x.shape, WIRE),
        in_specs=[SMEM, VMEM, pl.BlockSpec(memory_space=pltpu.HBM)],
        out_specs=VMEM,
        scratch_shapes=[
            pltpu.VMEM((N_HALF * N_COL + 1, width, size), FLOAT),
            pltpu.VMEM((N_COL + 1, width, size), FLOAT),
            pltpu.VMEM(blocks.shape, WIRE),
            pltpu.SemaphoreType.DMA((CHUNKS,)),
        ],
        compiler_params=pltpu.CompilerParams(vmem_limit_bytes=LARGE),
        name="terms",
    )(index, x, blocks)


def merge_kernel(got_ref, out_ref, acc):
    for h, b, z1, zh, q in places():
        piece = got_ref[0, b, h].astype(FLOAT)
        for k in range(1, N_Q):
            piece = piece + got_ref[k, b, h].astype(FLOAT)
        acc[z1, zh, q] = piece
    zh, z1 = lax.axis_index("zh"), lax.axis_index("z1")
    for q in range(N_Q):
        piece = got_ref[q, 0, N_HALF].astype(FLOAT)
        for b in range(1, N_COL):
            piece = piece + got_ref[q, b, N_HALF].astype(FLOAT)
        acc[z1, zh, q] = acc[z1, zh, q] + piece
    out_ref[...] = acc[...].astype(WIRE)


def merge(got):
    shape = (N_Z1, N_ZH, N_Q) + got.shape[3:]
    return pl.pallas_call(
        merge_kernel,
        out_shape=jax.ShapeDtypeStruct(shape, WIRE),
        in_specs=[VMEM],
        out_specs=VMEM,
        scratch_shapes=[pltpu.VMEM(shape, FLOAT)],
        compiler_params=pltpu.CompilerParams(vmem_limit_bytes=SMALL),
        name="merge",
    )(got)


def deal_kernel(all_ref, out_ref):
    zh, z1 = lax.axis_index("zh"), lax.axis_index("z1")
    for h, b, b_z1, b_zh, b_q in places():
        piece = all_ref[b_z1, b_zh, b_q]
        for q in range(N_Q):
            out_ref[q, b, h] = piece
    for q in range(N_Q):
        piece = all_ref[z1, zh, q]
        for b in range(N_COL):
            out_ref[q, b, N_HALF] = piece


def deal(pieces):
    return pl.pallas_call(
        deal_kernel,
        out_shape=jax.ShapeDtypeStruct((N_Q, N_COL, N_HALF + 1) + pieces.shape[3:], WIRE),
        in_specs=[VMEM],
        out_specs=VMEM,
        compiler_params=pltpu.CompilerParams(vmem_limit_bytes=SMALL),
        name="deal",
    )(pieces)


def exchange(x, axes):
    return lax.all_to_all(x, axes, 0, 0, tiled=True)


def total(x):
    return jnp.sum(x.astype(FLOAT), axis=0)


def local(vectors, blocks, slot_block_rows, slot_block_columns, counts):
    width, size = vectors.shape
    blocks = blocks[0, 0]
    rows = slot_block_rows[0, 0]
    cols = slot_block_columns[0, 0]
    slots = blocks.shape[0]
    row, col = lax.axis_index(ROW), lax.axis_index(COL)
    zh, z1 = lax.axis_index("zh"), lax.axis_index("z1")
    global_rows = row * N_COL + rows
    global_cols = (col + N_COL * (cols // N_COL)) * N_COL + cols % N_COL
    live = (jnp.arange(slots, dtype=jnp.int32) < counts[0, 0]) & (global_rows <= global_cols)
    index = jnp.concatenate([rows, cols, jnp.where(live, rows, N_COL), jnp.where(live, cols, N_HALF * N_COL)])

    def unit_sums(pieces):
        got = exchange(deal(pieces).reshape(N_Q * N_COL, N_HALF + 1, *pieces.shape[3:]), UNIT)
        out = terms(got.reshape(N_Q, N_COL, *got.shape[1:]), blocks, index)
        return merge(exchange(out.reshape(got.shape), UNIT).reshape(out.shape))

    quarter = exchange(vectors.reshape(N_Q, width // N_Q, size), QUAD)
    copies = jnp.broadcast_to(quarter.astype(WIRE)[None], (N_Z1 * N_ZH,) + quarter.shape)
    wire = exchange(copies, UNITS).reshape(N_Z1, N_ZH, *quarter.shape)
    before, now = None, wire[z1].astype(FLOAT).at[zh].set(quarter)
    for step in range(DEGREE - 1):
        pair_sums = total(exchange(unit_sums(wire), "z1")).astype(WIRE)
        image = total(lax.all_gather(pair_sums, "zh"))
        after = (image - CENTER * now) / HALF_WIDTH
        if step > 0:
            after = 2.0 * (image - CENTER * now) / HALF_WIDTH - before
        before, now = now, after
        wire = lax.all_gather(now.astype(WIRE), "z1")
    sums = unit_sums(wire)
    image = total(exchange(sums.reshape(-1, *sums.shape[2:]), UNITS))
    own = 2.0 * (image - CENTER * now[zh]) / HALF_WIDTH - before[zh]
    return exchange(own, QUAD).reshape(width, size)


def solution(mesh):
    split = Mesh(mesh.devices.reshape(N_ZH, N_Z1, 2, 2, 2, 4, 2), ALL)
    in_specs = (
        P(None, ALL),
        P(ROW, COL, None, None, None),
        P(ROW, COL, None),
        P(ROW, COL, None),
        P(ROW, COL),
    )
    return jax.shard_map(local, mesh=split, in_specs=in_specs, out_specs=P(None, ALL), check_vma=False)
```

```python
import functools

import jax
import jax.numpy as jnp
from jax import lax
from jax.experimental import pallas as pl
from jax.experimental.pallas import tpu as pltpu
from jax.sharding import Mesh, PartitionSpec as P

CENTER = 0.25
HALF_WIDTH = 2.0
DEGREE = 3
CHUNKS, AHEAD = 4, 2
QUAD = ("z0", "xl")
ROW = ("zh", "z1") + QUAD
COL = ("xh", "y", "core")
UNIT = QUAD + COL
SLABS = ("z1", "zh") + QUAD
ALL = ROW + COL
N_ZH, N_Z1, N_Q, N_COL = 4, 2, 4, 16
N_HALF = N_ZH * N_Z1 * N_Q // N_COL
VMEM = pl.BlockSpec(memory_space=pltpu.VMEM)
SMEM = pl.BlockSpec(memory_space=pltpu.SMEM)
FLOAT = jnp.float32
WIRE = jnp.bfloat16
SMALL, LARGE = 4 << 20, 52 << 20


def places():
    for h in range(N_HALF):
        for b in range(N_COL):
            zh, rest = divmod(h * N_COL + b, N_Z1 * N_Q)
            yield h, b, rest // N_Q, zh, rest % N_Q


def product(x, y, axis):
    return lax.dot_general(x, y, (((1,), (axis,)), ((), ())), preferred_element_type=FLOAT)


def terms_kernel(index, x_ref, blocks_hbm, out_ref, col_acc, row_acc, blocks, sems):
    slots, size = blocks.shape[:2]
    part = slots // CHUNKS
    width = x_ref.shape[0] * x_ref.shape[3]
    share = x_ref.shape[3]

    def copy(i):
        here = pl.ds(i * part, part)
        return pltpu.make_async_copy(blocks_hbm.at[here], blocks.at[here], sems.at[i])

    for i in range(AHEAD):
        copy(i).start()
    col_acc[...] = jnp.zeros_like(col_acc)
    row_acc[...] = jnp.zeros_like(row_acc)

    def chunk(i, carry):
        base = i * part
        copy(i).wait()

        @pl.when(i + AHEAD < CHUNKS)
        def _():
            copy(i + AHEAD).start()

        for s in range(0, part, 2):
            pair = (base + s, base + s + 1)
            both = [blocks[t] for t in pair]
            x_row = [x_ref[:, index[t], N_HALF].reshape(width, size) for t in pair]
            cols = [index[slots + t] for t in pair]
            x_col = [x_ref[:, lax.rem(c, N_COL), lax.div(c, N_COL)].reshape(width, size) for c in cols]
            by_col = product(jnp.concatenate(x_row), jnp.concatenate(both, axis=1), 0)
            by_row = product(jnp.concatenate(x_col), jnp.concatenate(both), 1)
            for i, t in enumerate(pair):
                own = (slice(i * width, (i + 1) * width), slice(i * size, (i + 1) * size))
                to = index[3 * slots + t]
                col_acc[to] = col_acc[to] + by_col[own]
                to = index[2 * slots + t]
                row_acc[to] = row_acc[to] + by_row[own]
        return carry

    lax.fori_loop(0, CHUNKS, chunk, 0)
    for k in range(x_ref.shape[0]):
        lines = slice(k * share, (k + 1) * share)
        for h in range(N_HALF):
            out_ref[k, :, h] = col_acc[h * N_COL : (h + 1) * N_COL, lines].astype(WIRE)
        out_ref[k, :, N_HALF] = row_acc[:N_COL, lines].astype(WIRE)


def terms(x, blocks, index):
    slots, size = blocks.shape[:2]
    width = x.shape[0] * x.shape[3]
    return pl.pallas_call(
        terms_kernel,
        out_shape=jax.ShapeDtypeStruct(x.shape, WIRE),
        in_specs=[SMEM, VMEM, pl.BlockSpec(memory_space=pltpu.HBM)],
        out_specs=VMEM,
        scratch_shapes=[
            pltpu.VMEM((N_HALF * N_COL + 1, width, size), FLOAT),
            pltpu.VMEM((N_COL + 1, width, size), FLOAT),
            pltpu.VMEM(blocks.shape, WIRE),
            pltpu.SemaphoreType.DMA((CHUNKS,)),
        ],
        compiler_params=pltpu.CompilerParams(vmem_limit_bytes=LARGE),
        name="terms",
    )(index, x, blocks)


def merge_kernel(extra_ref, got_ref, out_ref, acc):
    for h, b, z1, zh, q in places():
        piece = got_ref[0, b, h].astype(FLOAT)
        for k in range(1, N_Q):
            piece = piece + got_ref[k, b, h].astype(FLOAT)
        acc[z1, zh, q] = piece
    zh, z1 = lax.axis_index("zh"), lax.axis_index("z1")
    for q in range(N_Q):
        piece = got_ref[q, 0, N_HALF].astype(FLOAT)
        for b in range(1, N_COL):
            piece = piece + got_ref[q, b, N_HALF].astype(FLOAT)
        acc[z1, zh, q] = acc[z1, zh, q] + piece
    if extra_ref is not None:
        acc[z1, zh] = acc[z1, zh] + extra_ref[...]
    out_ref[...] = acc[...].astype(WIRE)


def merge(got, extra):
    shape = (N_Z1, N_ZH, N_Q) + got.shape[3:]
    given = [got] if extra is None else [extra, got]
    return pl.pallas_call(
        functools.partial(merge_kernel, None) if extra is None else merge_kernel,
        out_shape=jax.ShapeDtypeStruct(shape, WIRE),
        in_specs=[VMEM] * len(given),
        out_specs=VMEM,
        scratch_shapes=[pltpu.VMEM(shape, FLOAT)],
        compiler_params=pltpu.CompilerParams(vmem_limit_bytes=SMALL),
        name="merge",
    )(*given)


def deal_kernel(all_ref, out_ref):
    zh, z1 = lax.axis_index("zh"), lax.axis_index("z1")
    for h, b, b_z1, b_zh, b_q in places():
        piece = all_ref[b_z1, b_zh, b_q]
        for q in range(N_Q):
            out_ref[q, b, h] = piece
    for q in range(N_Q):
        piece = all_ref[z1, zh, q]
        for b in range(N_COL):
            out_ref[q, b, N_HALF] = piece


def deal(pieces):
    return pl.pallas_call(
        deal_kernel,
        out_shape=jax.ShapeDtypeStruct((N_Q, N_COL, N_HALF + 1) + pieces.shape[3:], WIRE),
        in_specs=[VMEM],
        out_specs=VMEM,
        compiler_params=pltpu.CompilerParams(vmem_limit_bytes=SMALL),
        name="deal",
    )(pieces)


def exchange(x, axes):
    return lax.all_to_all(x, axes, 0, 0, tiled=True)


def total(x):
    return jnp.sum(x.astype(FLOAT), axis=0)


def local(vectors, blocks, slot_block_rows, slot_block_columns, counts):
    width, size = vectors.shape
    blocks = blocks[0, 0]
    rows = slot_block_rows[0, 0]
    cols = slot_block_columns[0, 0]
    slots = blocks.shape[0]
    row, col = lax.axis_index(ROW), lax.axis_index(COL)
    zh, z1 = lax.axis_index("zh"), lax.axis_index("z1")
    global_rows = row * N_COL + rows
    global_cols = (col + N_COL * (cols // N_COL)) * N_COL + cols % N_COL
    live = (jnp.arange(slots, dtype=jnp.int32) < counts[0, 0]) & (global_rows <= global_cols)
    index = jnp.concatenate([rows, cols, jnp.where(live, rows, N_COL), jnp.where(live, cols, N_HALF * N_COL)])

    def unit_sums(pieces, extra=None):
        got = exchange(deal(pieces).reshape(N_Q * N_COL, N_HALF + 1, *pieces.shape[3:]), UNIT)
        out = terms(got.reshape(N_Q, N_COL, *got.shape[1:]), blocks, index)
        return merge(exchange(out.reshape(got.shape), UNIT).reshape(out.shape), extra)

    quarters = vectors.astype(WIRE).reshape(1, N_Q, width // N_Q, size)
    copies = jnp.broadcast_to(quarters, (N_Z1 * N_ZH,) + quarters.shape[1:]).reshape(-1, *quarters.shape[2:])
    wire = exchange(copies, SLABS).reshape(N_Z1, N_ZH, *quarters.shape[1:])
    before, now = None, wire[z1].astype(FLOAT)
    for step in range(DEGREE - 1):
        pair_sums = total(exchange(unit_sums(wire), "z1")).astype(WIRE)
        image = total(lax.all_gather(pair_sums, "zh"))
        after = (image - CENTER * now) / HALF_WIDTH
        if step > 0:
            after = 2.0 * (image - CENTER * now) / HALF_WIDTH - before
        before, now = now, after
        wire = lax.all_gather(now.astype(WIRE), "z1")
    sums = unit_sums(wire, -(CENTER * now[zh] + HALF_WIDTH / 2.0 * before[zh]))
    got = exchange(sums.reshape(-1, *sums.shape[3:]), SLABS).reshape(N_Z1 * N_ZH, *quarters.shape[1:])
    return (2.0 * total(got) / HALF_WIDTH).reshape(width, size)


def solution(mesh):
    split = Mesh(mesh.devices.reshape(N_ZH, N_Z1, 2, 2, 2, 4, 2), ALL)
    in_specs = (
        P(None, ALL),
        P(ROW, COL, None, None, None),
        P(ROW, COL, None),
        P(ROW, COL, None),
        P(ROW, COL),
    )
    return jax.shard_map(local, mesh=split, in_specs=in_specs, out_specs=P(None, ALL), check_vma=False)
```

```python
import functools

import jax
import jax.numpy as jnp
from jax import lax
from jax.experimental import pallas as pl
from jax.experimental.pallas import tpu as pltpu
from jax.sharding import Mesh, PartitionSpec as P

CENTER = 0.25
HALF_WIDTH = 2.0
DEGREE = 3
CHUNKS, AHEAD = 4, 2
QUAD = ("z0", "xl")
ROW = ("zh", "z1") + QUAD
COL = ("xh", "y", "core")
UNIT = QUAD + COL
SLABS = ("z1", "zh") + QUAD
ALL = ROW + COL
N_ZH, N_Z1, N_Q, N_COL = 4, 2, 4, 16
N_HALF = N_ZH * N_Z1 * N_Q // N_COL
VMEM = pl.BlockSpec(memory_space=pltpu.VMEM)
SMEM = pl.BlockSpec(memory_space=pltpu.SMEM)
FLOAT = jnp.float32
WIRE = jnp.bfloat16
SMALL, LARGE = 4 << 20, 52 << 20


def places():
    for h in range(N_HALF):
        for b in range(N_COL):
            zh, rest = divmod(h * N_COL + b, N_Z1 * N_Q)
            yield h, b, rest // N_Q, zh, rest % N_Q


def product(x, y, axis):
    return lax.dot_general(x, y, (((1,), (axis,)), ((), ())), preferred_element_type=FLOAT)


def terms_kernel(index, x_ref, blocks_hbm, out_ref, col_acc, row_acc, blocks, sems):
    slots, size = blocks.shape[:2]
    part = slots // CHUNKS
    width = x_ref.shape[0] * x_ref.shape[3]
    share = x_ref.shape[3]

    def copy(i):
        here = pl.ds(i * part, part)
        return pltpu.make_async_copy(blocks_hbm.at[here], blocks.at[here], sems.at[i])

    for i in range(AHEAD):
        copy(i).start()
    col_acc[...] = jnp.zeros_like(col_acc)
    row_acc[...] = jnp.zeros_like(row_acc)

    def chunk(i, carry):
        base = i * part
        copy(i).wait()

        @pl.when(i + AHEAD < CHUNKS)
        def _():
            copy(i + AHEAD).start()

        for s in range(0, part, 2):
            pair = (base + s, base + s + 1)
            both = [blocks[t] for t in pair]
            x_row = [x_ref[:, index[t], N_HALF].reshape(width, size) for t in pair]
            cols = [index[slots + t] for t in pair]
            x_col = [x_ref[:, lax.rem(c, N_COL), lax.div(c, N_COL)].reshape(width, size) for c in cols]
            by_col = product(jnp.concatenate(x_row), jnp.concatenate(both, axis=1), 0)
            by_row = product(jnp.concatenate(x_col), jnp.concatenate(both), 1)
            for i, t in enumerate(pair):
                own = (slice(i * width, (i + 1) * width), slice(i * size, (i + 1) * size))
                to = index[3 * slots + t]
                col_acc[to] = col_acc[to] + by_col[own]
                to = index[2 * slots + t]
                row_acc[to] = row_acc[to] + by_row[own]
        return carry

    lax.fori_loop(0, CHUNKS, chunk, 0)
    for k in range(x_ref.shape[0]):
        lines = slice(k * share, (k + 1) * share)
        for h in range(N_HALF):
            out_ref[k, :, h] = col_acc[h * N_COL : (h + 1) * N_COL, lines].astype(WIRE)
        out_ref[k, :, N_HALF] = row_acc[:N_COL, lines].astype(WIRE)


def terms(x, blocks, index):
    slots, size = blocks.shape[:2]
    width = x.shape[0] * x.shape[3]
    return pl.pallas_call(
        terms_kernel,
        out_shape=jax.ShapeDtypeStruct(x.shape, WIRE),
        in_specs=[SMEM, VMEM, pl.BlockSpec(memory_space=pltpu.HBM)],
        out_specs=VMEM,
        scratch_shapes=[
            pltpu.VMEM((N_HALF * N_COL + 1, width, size), FLOAT),
            pltpu.VMEM((N_COL + 1, width, size), FLOAT),
            pltpu.VMEM(blocks.shape, WIRE),
            pltpu.SemaphoreType.DMA((CHUNKS,)),
        ],
        compiler_params=pltpu.CompilerParams(vmem_limit_bytes=LARGE),
        name="terms",
    )(index, x, blocks)


def merge_kernel(last, got_ref, *refs):
    acc = refs[-1]
    for h, b, z1, zh, q in places():
        piece = got_ref[0, b, h].astype(FLOAT)
        for k in range(1, N_Q):
            piece = piece + got_ref[k, b, h].astype(FLOAT)
        acc[z1, zh, q] = piece
    zh, z1 = lax.axis_index("zh"), lax.axis_index("z1")
    for q in range(N_Q):
        piece = got_ref[q, 0, N_HALF].astype(FLOAT)
        for b in range(1, N_COL):
            piece = piece + got_ref[q, b, N_HALF].astype(FLOAT)
        acc[z1, zh, q] = acc[z1, zh, q] + piece
    if last:
        extra_ref, out_ref = refs[:2]
        acc[z1, zh] = acc[z1, zh] + extra_ref[...]
        out_ref[...] = acc[...].astype(WIRE)
    else:
        kept_ref, sent_ref = refs[:2]
        kept_ref[...] = acc[z1]
        sent_ref[...] = acc[1 - z1].astype(WIRE)


def merge(got, extra):
    shape = (N_Z1, N_ZH, N_Q) + got.shape[3:]
    last = extra is not None
    kept, sent = jax.ShapeDtypeStruct(shape[1:], FLOAT), jax.ShapeDtypeStruct(shape[1:], WIRE)
    return pl.pallas_call(
        functools.partial(merge_kernel, last),
        out_shape=jax.ShapeDtypeStruct(shape, WIRE) if last else (kept, sent),
        in_specs=[VMEM] * (2 if last else 1),
        out_specs=VMEM if last else (VMEM, VMEM),
        scratch_shapes=[pltpu.VMEM(shape, FLOAT)],
        compiler_params=pltpu.CompilerParams(vmem_limit_bytes=SMALL),
        name="merge",
    )(*((got, extra) if last else (got,)))


def deal_kernel(all_ref, out_ref):
    zh, z1 = lax.axis_index("zh"), lax.axis_index("z1")
    for h, b, b_z1, b_zh, b_q in places():
        piece = all_ref[b_z1, b_zh, b_q]
        for q in range(N_Q):
            out_ref[q, b, h] = piece
    for q in range(N_Q):
        piece = all_ref[z1, zh, q]
        for b in range(N_COL):
            out_ref[q, b, N_HALF] = piece


def deal(pieces):
    return pl.pallas_call(
        deal_kernel,
        out_shape=jax.ShapeDtypeStruct((N_Q, N_COL, N_HALF + 1) + pieces.shape[3:], WIRE),
        in_specs=[VMEM],
        out_specs=VMEM,
        compiler_params=pltpu.CompilerParams(vmem_limit_bytes=SMALL),
        name="deal",
    )(pieces)


def exchange(x, axes):
    return lax.all_to_all(x, axes, 0, 0, tiled=True)


def total(x):
    return jnp.sum(x.astype(FLOAT), axis=0)


def local(vectors, blocks, slot_block_rows, slot_block_columns, counts):
    width, size = vectors.shape
    blocks = blocks[0, 0]
    rows = slot_block_rows[0, 0]
    cols = slot_block_columns[0, 0]
    slots = blocks.shape[0]
    row, col = lax.axis_index(ROW), lax.axis_index(COL)
    zh, z1 = lax.axis_index("zh"), lax.axis_index("z1")
    global_rows = row * N_COL + rows
    global_cols = (col + N_COL * (cols // N_COL)) * N_COL + cols % N_COL
    live = (jnp.arange(slots, dtype=jnp.int32) < counts[0, 0]) & (global_rows <= global_cols)
    index = jnp.concatenate([rows, cols, jnp.where(live, rows, N_COL), jnp.where(live, cols, N_HALF * N_COL)])

    def unit_sums(pieces, extra=None):
        got = exchange(deal(pieces).reshape(N_Q * N_COL, N_HALF + 1, *pieces.shape[3:]), UNIT)
        out = terms(got.reshape(N_Q, N_COL, *got.shape[1:]), blocks, index)
        return merge(exchange(out.reshape(got.shape), UNIT).reshape(out.shape), extra)

    quarters = vectors.astype(WIRE).reshape(1, N_Q, width // N_Q, size)
    copies = jnp.broadcast_to(quarters, (N_Z1 * N_ZH,) + quarters.shape[1:]).reshape(-1, *quarters.shape[2:])
    wire = exchange(copies, SLABS).reshape(N_Z1, N_ZH, *quarters.shape[1:])
    before, now = None, wire[z1].astype(FLOAT)
    for step in range(DEGREE - 1):
        kept, sent = unit_sums(wire)
        pair_sums = kept + lax.ppermute(sent, "z1", [(0, 1), (1, 0)]).astype(FLOAT)
        image = total(lax.all_gather(pair_sums.astype(WIRE), "zh"))
        after = (image - CENTER * now) / HALF_WIDTH
        if step > 0:
            after = 2.0 * (image - CENTER * now) / HALF_WIDTH - before
        before, now = now, after
        wire = lax.all_gather(now.astype(WIRE), "z1")
    sums = unit_sums(wire, -(CENTER * now[zh] + HALF_WIDTH / 2.0 * before[zh]))
    got = exchange(sums.reshape(-1, *sums.shape[3:]), SLABS).reshape(N_Z1 * N_ZH, *quarters.shape[1:])
    return (2.0 * total(got) / HALF_WIDTH).reshape(width, size)


def solution(mesh):
    split = Mesh(mesh.devices.reshape(N_ZH, N_Z1, 2, 2, 2, 4, 2), ALL)
    in_specs = (
        P(None, ALL),
        P(ROW, COL, None, None, None),
        P(ROW, COL, None),
        P(ROW, COL, None),
        P(ROW, COL),
    )
    return jax.shard_map(local, mesh=split, in_specs=in_specs, out_specs=P(None, ALL), check_vma=False)
```

```python
import functools

import jax
import jax.numpy as jnp
from jax import lax
from jax.experimental import pallas as pl
from jax.experimental.pallas import tpu as pltpu
from jax.sharding import Mesh, PartitionSpec as P

CENTER = 0.25
HALF_WIDTH = 2.0
DEGREE = 3
CHUNKS, AHEAD = 4, 2
QUAD = ("z0", "xl")
ROW = ("zh", "z1") + QUAD
COL = ("xh", "y", "core")
UNIT = QUAD + COL
SLABS = ("z1", "zh") + QUAD
ALL = ROW + COL
N_ZH, N_Z1, N_Q, N_COL = 4, 2, 4, 16
N_HALF = N_ZH * N_Z1 * N_Q // N_COL
VMEM = pl.BlockSpec(memory_space=pltpu.VMEM)
SMEM = pl.BlockSpec(memory_space=pltpu.SMEM)
FLOAT = jnp.float32
WIRE = jnp.bfloat16
SMALL, LARGE = 4 << 20, 52 << 20


def places():
    for h in range(N_HALF):
        for b in range(N_COL):
            zh, rest = divmod(h * N_COL + b, N_Z1 * N_Q)
            yield h, b, rest // N_Q, zh, rest % N_Q


def product(x, y, axis):
    return lax.dot_general(x, y, (((1,), (axis,)), ((), ())), preferred_element_type=FLOAT)


def terms_kernel(index, x_ref, blocks_hbm, out_ref, col_acc, row_acc, blocks, sems):
    slots, size = blocks.shape[:2]
    part = slots // CHUNKS
    width = x_ref.shape[0] * x_ref.shape[3]
    share = x_ref.shape[3]

    def copy(i):
        here = pl.ds(i * part, part)
        return pltpu.make_async_copy(blocks_hbm.at[here], blocks.at[here], sems.at[i])

    for i in range(AHEAD):
        copy(i).start()
    col_acc[...] = jnp.zeros_like(col_acc)
    row_acc[...] = jnp.zeros_like(row_acc)

    def chunk(i, carry):
        base = i * part
        copy(i).wait()

        @pl.when(i + AHEAD < CHUNKS)
        def _():
            copy(i + AHEAD).start()

        for s in range(0, part, 2):
            pair = (base + s, base + s + 1)
            both = [blocks[t] for t in pair]
            x_row = [x_ref[:, index[t], N_HALF].reshape(width, size) for t in pair]
            cols = [index[slots + t] for t in pair]
            x_col = [x_ref[:, lax.rem(c, N_COL), lax.div(c, N_COL)].reshape(width, size) for c in cols]
            by_col = product(jnp.concatenate(x_row), jnp.concatenate(both, axis=1), 0)
            by_row = product(jnp.concatenate(x_col), jnp.concatenate(both), 1)
            for i, t in enumerate(pair):
                own = (slice(i * width, (i + 1) * width), slice(i * size, (i + 1) * size))
                to = index[3 * slots + t]
                col_acc[to] = col_acc[to] + by_col[own]
                to = index[2 * slots + t]
                row_acc[to] = row_acc[to] + by_row[own]
        return carry

    lax.fori_loop(0, CHUNKS, chunk, 0)
    for k in range(x_ref.shape[0]):
        lines = slice(k * share, (k + 1) * share)
        for h in range(N_HALF):
            out_ref[k, :, h] = col_acc[h * N_COL : (h + 1) * N_COL, lines].astype(WIRE)
        out_ref[k, :, N_HALF] = row_acc[:N_COL, lines].astype(WIRE)


def terms(x, blocks, index):
    slots, size = blocks.shape[:2]
    width = x.shape[0] * x.shape[3]
    return pl.pallas_call(
        terms_kernel,
        out_shape=jax.ShapeDtypeStruct(x.shape, WIRE),
        in_specs=[SMEM, VMEM, pl.BlockSpec(memory_space=pltpu.HBM)],
        out_specs=VMEM,
        scratch_shapes=[
            pltpu.VMEM((N_HALF * N_COL + 1, width, size), FLOAT),
            pltpu.VMEM((N_COL + 1, width, size), FLOAT),
            pltpu.VMEM(blocks.shape, WIRE),
            pltpu.SemaphoreType.DMA((CHUNKS,)),
        ],
        compiler_params=pltpu.CompilerParams(vmem_limit_bytes=LARGE),
        name="terms",
    )(index, x, blocks)


def merge_kernel(last, got_ref, *refs):
    acc = refs[-1]
    for h, b, z1, zh, q in places():
        piece = got_ref[0, b, h].astype(FLOAT)
        for k in range(1, N_Q):
            piece = piece + got_ref[k, b, h].astype(FLOAT)
        acc[z1, zh, q] = piece
    zh, z1 = lax.axis_index("zh"), lax.axis_index("z1")
    for q in range(N_Q):
        piece = got_ref[q, 0, N_HALF].astype(FLOAT)
        for b in range(1, N_COL):
            piece = piece + got_ref[q, b, N_HALF].astype(FLOAT)
        acc[z1, zh, q] = acc[z1, zh, q] + piece
    if last:
        extra_ref, out_ref = refs[:2]
        acc[z1, zh] = acc[z1, zh] + extra_ref[...]
        out_ref[...] = acc[...].astype(WIRE)
    else:
        kept_ref, sent_ref = refs[:2]
        kept_ref[...] = acc[z1]
        sent_ref[...] = acc[1 - z1].astype(WIRE)


def merge(got, extra):
    shape = (N_Z1, N_ZH, N_Q) + got.shape[3:]
    last = extra is not None
    kept, sent = jax.ShapeDtypeStruct(shape[1:], FLOAT), jax.ShapeDtypeStruct(shape[1:], WIRE)
    return pl.pallas_call(
        functools.partial(merge_kernel, last),
        out_shape=jax.ShapeDtypeStruct(shape, WIRE) if last else (kept, sent),
        in_specs=[VMEM] * (2 if last else 1),
        out_specs=VMEM if last else (VMEM, VMEM),
        scratch_shapes=[pltpu.VMEM(shape, FLOAT)],
        compiler_params=pltpu.CompilerParams(vmem_limit_bytes=SMALL),
        name="merge",
    )(*((got, extra) if last else (got,)))


def deal_kernel(all_ref, out_ref):
    zh, z1 = lax.axis_index("zh"), lax.axis_index("z1")
    for h, b, b_z1, b_zh, b_q in places():
        piece = all_ref[b_z1, b_zh, b_q]
        for q in range(N_Q):
            out_ref[q, b, h] = piece
    for q in range(N_Q):
        piece = all_ref[z1, zh, q]
        for b in range(N_COL):
            out_ref[q, b, N_HALF] = piece


def deal(pieces):
    return pl.pallas_call(
        deal_kernel,
        out_shape=jax.ShapeDtypeStruct((N_Q, N_COL, N_HALF + 1) + pieces.shape[3:], WIRE),
        in_specs=[VMEM],
        out_specs=VMEM,
        compiler_params=pltpu.CompilerParams(vmem_limit_bytes=SMALL),
        name="deal",
    )(pieces)


def exchange(x, axes):
    return lax.all_to_all(x, axes, 0, 0, tiled=True)


def total(x):
    return jnp.sum(x.astype(FLOAT), axis=0)


def local(vectors, blocks, slot_block_rows, slot_block_columns, counts):
    width, size = vectors.shape
    blocks = blocks[0, 0]
    rows = slot_block_rows[0, 0]
    cols = slot_block_columns[0, 0]
    slots = blocks.shape[0]
    row, col = lax.axis_index(ROW), lax.axis_index(COL)
    zh, z1 = lax.axis_index("zh"), lax.axis_index("z1")
    global_rows = row * N_COL + rows
    global_cols = (col + N_COL * (cols // N_COL)) * N_COL + cols % N_COL
    live = (jnp.arange(slots, dtype=jnp.int32) < counts[0, 0]) & (global_rows <= global_cols)
    index = jnp.concatenate([rows, cols, jnp.where(live, rows, N_COL), jnp.where(live, cols, N_HALF * N_COL)])

    def unit_sums(pieces, extra=None):
        got = exchange(deal(pieces).reshape(N_Q * N_COL, N_HALF + 1, *pieces.shape[3:]), UNIT)
        out = terms(got.reshape(N_Q, N_COL, *got.shape[1:]), blocks, index)
        return merge(exchange(out.reshape(got.shape), UNIT).reshape(out.shape), extra)

    quarters = vectors.astype(WIRE).reshape(1, N_Q, width // N_Q, size)
    copies = jnp.broadcast_to(quarters, (N_Z1 * N_ZH,) + quarters.shape[1:]).reshape(-1, *quarters.shape[2:])
    wire = exchange(copies, SLABS).reshape(N_Z1, N_ZH, *quarters.shape[1:])
    before, now = None, wire[z1].astype(FLOAT)
    for step in range(DEGREE - 1):
        kept, sent = unit_sums(wire)
        pair_sums = kept + lax.ppermute(sent, "z1", [(0, 1), (1, 0)]).astype(FLOAT)
        far = total(lax.all_gather(pair_sums[1:].astype(WIRE), "zh"))
        image = jnp.concatenate([pair_sums[:1], far])
        after = (image - CENTER * now) / HALF_WIDTH
        if step > 0:
            after = 2.0 * (image - CENTER * now) / HALF_WIDTH - before
        before, now = now, after
        wire = lax.all_gather(now.astype(WIRE), "z1")
    sums = unit_sums(wire, -(CENTER * now[zh] + HALF_WIDTH / 2.0 * before[zh]))
    got = exchange(sums.reshape(-1, *sums.shape[3:]), SLABS).reshape(N_Z1 * N_ZH, *quarters.shape[1:])
    return (2.0 * total(got) / HALF_WIDTH).reshape(width, size)


def solution(mesh):
    split = Mesh(mesh.devices.reshape(N_ZH, N_Z1, 2, 2, 2, 4, 2), ALL)
    in_specs = (
        P(None, ALL),
        P(ROW, COL, None, None, None),
        P(ROW, COL, None),
        P(ROW, COL, None),
        P(ROW, COL),
    )
    return jax.shard_map(local, mesh=split, in_specs=in_specs, out_specs=P(None, ALL), check_vma=False)
```

```python
import functools

import jax
import jax.numpy as jnp
from jax import lax
from jax.experimental import pallas as pl
from jax.experimental.pallas import tpu as pltpu
from jax.sharding import Mesh, PartitionSpec as P

CENTER = 0.25
HALF_WIDTH = 2.0
DEGREE = 3
FIRST, CHUNKS, AHEAD = 8, 5, 2
QUAD = ("z0", "xl")
ROW = ("zh", "z1") + QUAD
COL = ("xh", "y", "core")
UNIT = QUAD + COL
SLABS = ("z1", "zh") + QUAD
ALL = ROW + COL
N_ZH, N_Z1, N_Q, N_COL = 4, 2, 4, 16
N_HALF = N_ZH * N_Z1 * N_Q // N_COL
VMEM = pl.BlockSpec(memory_space=pltpu.VMEM)
SMEM = pl.BlockSpec(memory_space=pltpu.SMEM)
FLOAT = jnp.float32
WIRE = jnp.bfloat16
SMALL, LARGE = 4 << 20, 52 << 20


def places():
    for h in range(N_HALF):
        for b in range(N_COL):
            zh, rest = divmod(h * N_COL + b, N_Z1 * N_Q)
            yield h, b, rest // N_Q, zh, rest % N_Q


def product(x, y, axis):
    return lax.dot_general(x, y, (((1,), (axis,)), ((), ())), preferred_element_type=FLOAT)


def terms_kernel(index, x_ref, blocks_hbm, out_ref, col_acc, row_acc, blocks, sems):
    slots, size = blocks.shape[:2]
    part = (slots - FIRST) // (CHUNKS - 1)
    width = x_ref.shape[0] * x_ref.shape[3]
    share = x_ref.shape[3]

    def copy(i):
        here = pl.ds(0, FIRST) if isinstance(i, int) and i == 0 else pl.ds(FIRST + (i - 1) * part, part)
        return pltpu.make_async_copy(blocks_hbm.at[here], blocks.at[here], sems.at[i])

    def work(base, count):
        for s in range(0, count, 2):
            pair = (base + s, base + s + 1)
            both = [blocks[t] for t in pair]
            x_row = [x_ref[:, index[t], N_HALF].reshape(width, size) for t in pair]
            cols = [index[slots + t] for t in pair]
            x_col = [x_ref[:, lax.rem(c, N_COL), lax.div(c, N_COL)].reshape(width, size) for c in cols]
            by_col = product(jnp.concatenate(x_row), jnp.concatenate(both, axis=1), 0)
            by_row = product(jnp.concatenate(x_col), jnp.concatenate(both), 1)
            for i, t in enumerate(pair):
                own = (slice(i * width, (i + 1) * width), slice(i * size, (i + 1) * size))
                to = index[3 * slots + t]
                col_acc[to] = col_acc[to] + by_col[own]
                to = index[2 * slots + t]
                row_acc[to] = row_acc[to] + by_row[own]

    for i in range(AHEAD + 1):
        copy(i).start()
    col_acc[...] = jnp.zeros_like(col_acc)
    row_acc[...] = jnp.zeros_like(row_acc)
    copy(0).wait()
    work(0, FIRST)

    def chunk(i, carry):
        copy(i).wait()

        @pl.when(i + AHEAD < CHUNKS)
        def _():
            copy(i + AHEAD).start()

        work(FIRST + (i - 1) * part, part)
        return carry

    lax.fori_loop(1, CHUNKS, chunk, 0)
    for k in range(x_ref.shape[0]):
        lines = slice(k * share, (k + 1) * share)
        for h in range(N_HALF):
            out_ref[k, :, h] = col_acc[h * N_COL : (h + 1) * N_COL, lines].astype(WIRE)
        out_ref[k, :, N_HALF] = row_acc[:N_COL, lines].astype(WIRE)


def terms(x, blocks, index):
    slots, size = blocks.shape[:2]
    width = x.shape[0] * x.shape[3]
    return pl.pallas_call(
        terms_kernel,
        out_shape=jax.ShapeDtypeStruct(x.shape, WIRE),
        in_specs=[SMEM, VMEM, pl.BlockSpec(memory_space=pltpu.HBM)],
        out_specs=VMEM,
        scratch_shapes=[
            pltpu.VMEM((N_HALF * N_COL + 1, width, size), FLOAT),
            pltpu.VMEM((N_COL + 1, width, size), FLOAT),
            pltpu.VMEM(blocks.shape, WIRE),
            pltpu.SemaphoreType.DMA((CHUNKS,)),
        ],
        compiler_params=pltpu.CompilerParams(vmem_limit_bytes=LARGE),
        name="terms",
    )(index, x, blocks)


def merge_kernel(last, got_ref, *refs):
    acc = refs[-1]
    for h, b, z1, zh, q in places():
        piece = got_ref[0, b, h].astype(FLOAT)
        for k in range(1, N_Q):
            piece = piece + got_ref[k, b, h].astype(FLOAT)
        acc[z1, zh, q] = piece
    zh, z1 = lax.axis_index("zh"), lax.axis_index("z1")
    for q in range(N_Q):
        piece = got_ref[q, 0, N_HALF].astype(FLOAT)
        for b in range(1, N_COL):
            piece = piece + got_ref[q, b, N_HALF].astype(FLOAT)
        acc[z1, zh, q] = acc[z1, zh, q] + piece
    if last:
        extra_ref, out_ref = refs[:2]
        acc[z1, zh] = acc[z1, zh] + extra_ref[...]
        out_ref[...] = acc[...].astype(WIRE)
    else:
        kept_ref, sent_ref = refs[:2]
        kept_ref[...] = acc[z1]
        sent_ref[...] = acc[1 - z1].astype(WIRE)


def merge(got, extra):
    shape = (N_Z1, N_ZH, N_Q) + got.shape[3:]
    last = extra is not None
    kept, sent = jax.ShapeDtypeStruct(shape[1:], FLOAT), jax.ShapeDtypeStruct(shape[1:], WIRE)
    return pl.pallas_call(
        functools.partial(merge_kernel, last),
        out_shape=jax.ShapeDtypeStruct(shape, WIRE) if last else (kept, sent),
        in_specs=[VMEM] * (2 if last else 1),
        out_specs=VMEM if last else (VMEM, VMEM),
        scratch_shapes=[pltpu.VMEM(shape, FLOAT)],
        compiler_params=pltpu.CompilerParams(vmem_limit_bytes=SMALL),
        name="merge",
    )(*((got, extra) if last else (got,)))


def deal_kernel(all_ref, out_ref):
    zh, z1 = lax.axis_index("zh"), lax.axis_index("z1")
    for h, b, b_z1, b_zh, b_q in places():
        piece = all_ref[b_z1, b_zh, b_q]
        for q in range(N_Q):
            out_ref[q, b, h] = piece
    for q in range(N_Q):
        piece = all_ref[z1, zh, q]
        for b in range(N_COL):
            out_ref[q, b, N_HALF] = piece


def deal(pieces):
    return pl.pallas_call(
        deal_kernel,
        out_shape=jax.ShapeDtypeStruct((N_Q, N_COL, N_HALF + 1) + pieces.shape[3:], WIRE),
        in_specs=[VMEM],
        out_specs=VMEM,
        compiler_params=pltpu.CompilerParams(vmem_limit_bytes=SMALL),
        name="deal",
    )(pieces)


def exchange(x, axes):
    return lax.all_to_all(x, axes, 0, 0, tiled=True)


def total(x):
    return jnp.sum(x.astype(FLOAT), axis=0)


def local(vectors, blocks, slot_block_rows, slot_block_columns, counts):
    width, size = vectors.shape
    blocks = blocks[0, 0]
    rows = slot_block_rows[0, 0]
    cols = slot_block_columns[0, 0]
    slots = blocks.shape[0]
    row, col = lax.axis_index(ROW), lax.axis_index(COL)
    zh, z1 = lax.axis_index("zh"), lax.axis_index("z1")
    global_rows = row * N_COL + rows
    global_cols = (col + N_COL * (cols // N_COL)) * N_COL + cols % N_COL
    live = (jnp.arange(slots, dtype=jnp.int32) < counts[0, 0]) & (global_rows <= global_cols)
    index = jnp.concatenate([rows, cols, jnp.where(live, rows, N_COL), jnp.where(live, cols, N_HALF * N_COL)])

    def unit_sums(pieces, extra=None):
        got = exchange(deal(pieces).reshape(N_Q * N_COL, N_HALF + 1, *pieces.shape[3:]), UNIT)
        out = terms(got.reshape(N_Q, N_COL, *got.shape[1:]), blocks, index)
        return merge(exchange(out.reshape(got.shape), UNIT).reshape(out.shape), extra)

    quarters = vectors.astype(WIRE).reshape(1, N_Q, width // N_Q, size)
    copies = jnp.broadcast_to(quarters, (N_Z1 * N_ZH,) + quarters.shape[1:]).reshape(-1, *quarters.shape[2:])
    wire = exchange(copies, SLABS).reshape(N_Z1, N_ZH, *quarters.shape[1:])
    before, now = None, wire[z1].astype(FLOAT)
    for step in range(DEGREE - 1):
        kept, sent = unit_sums(wire)
        pair_sums = kept + lax.ppermute(sent, "z1", [(0, 1), (1, 0)]).astype(FLOAT)
        far = total(lax.all_gather(pair_sums[1:].astype(WIRE), "zh"))
        image = jnp.concatenate([pair_sums[:1], far])
        after = (image - CENTER * now) / HALF_WIDTH
        if step > 0:
            after = 2.0 * (image - CENTER * now) / HALF_WIDTH - before
        before, now = now, after
        wire = lax.all_gather(now.astype(WIRE), "z1")
    sums = unit_sums(wire, -(CENTER * now[zh] + HALF_WIDTH / 2.0 * before[zh]))
    got = exchange(sums.reshape(-1, *sums.shape[3:]), SLABS).reshape(N_Z1 * N_ZH, *quarters.shape[1:])
    return (2.0 * total(got) / HALF_WIDTH).reshape(width, size)


def solution(mesh):
    split = Mesh(mesh.devices.reshape(N_ZH, N_Z1, 2, 2, 2, 4, 2), ALL)
    in_specs = (
        P(None, ALL),
        P(ROW, COL, None, None, None),
        P(ROW, COL, None),
        P(ROW, COL, None),
        P(ROW, COL),
    )
    return jax.shard_map(local, mesh=split, in_specs=in_specs, out_specs=P(None, ALL), check_vma=False)
```
